32 devices in a mesh: dp: 8 (over y, x, core), fsdp: 4 (over z).
Axes of the slice: x: 2, y: 2, z: 4, core: 2. Of those that a mesh axis runs over, the one named last changes fastest.
Arguments:
- latents: bfloat16 [8, 2, 256, 2432], P('dp', None, 'fsdp'), may hold values from -6 to 6
- targets: bfloat16 [8, 2, 256, 2432], P('dp', None, 'fsdp'), may hold values from -6 to 6
- frozen_weight: bfloat16 [2432, 2432], P('fsdp'), may hold values from -0.125 to 0.125
- adapter_down: bfloat16 [7, 64, 2432], P(None, None, 'dp'), may hold values from -0.125 to 0.125
- adapter_up: bfloat16 [7, 64, 2432], P(None, None, 'dp'), may hold values from -0.75 to 0.75
- categories: int32 [8], P('dp'), may hold values from 0 to 6
- timesteps: int32 [8], P('dp'), may hold values from 0 to 999
Outputs:
- grad_down: float32 [7, 64, 2432], P(None, None, 'dp')
- grad_up: float32 [7, 64, 2432], P(None, None, 'dp')
- losses: float32 [8], P('dp')
The draws below stay inside these ranges and needn't reach their ends.
All inputs are finite; a program needn't handle non-finite values.
Results may differ from the reference program's by a relative error of at most 0.0048.
Values may be sent and summed in bfloat16 or wider, within the bound.
A program may use at most 128 MiB of HBM per device.

```python
import math
import jax
import jax.numpy as jnp
import numpy as np
from jax import lax

MODEL_WIDTH = 2432
ADAPTER_RANK = 64
HARM_CLASSES = 7
TOKENS = 256
PAIRS = 8


def set_ends(values, stream_key, least, largest):
    dims = values.shape
    spot = [jax.random.randint(jax.random.fold_in(stream_key, axis), (), 0, dims[axis]) for axis in range(len(dims))]
    values = values.at[tuple(spot)].set(least)
    longest = dims.index(max(dims))
    spot[longest] = (spot[longest] + 1) % dims[longest]
    return values.at[tuple(spot)].set(largest)


def levels(stream_key, dims, pieces, least, top_value):
    def one(position, parts):
        heights = jax.random.uniform(jax.random.fold_in(jax.random.fold_in(stream_key, 6), position), (parts,), jnp.float32, least / len(pieces), top_value / len(pieces))
        return jnp.repeat(jnp.exp(heights), dims[position] // parts).reshape((-1,) + (1,) * (len(dims) - position - 1))

    factor_of = one(*pieces[0])
    for cut in pieces[1:]:
        factor_of = factor_of * one(*cut)
    return factor_of


def rank_table(number_of, slope):
    portions = [(1 << 20) // math.isqrt(grade ** slope) + 1 for grade in range(1, number_of + 1)]
    spread = 1 + sum(portions) // (1 << 30)
    return np.cumsum(np.array([max(1, weight // spread) for weight in portions]))


def ranked_ids(key, shape, number_of, lean):
    grid = rank_table(number_of, lean)
    lot = jax.random.randint(jax.random.fold_in(key, 1), shape, 0, int(grid[number_of - 1]))
    grade = jnp.searchsorted(jnp.asarray(grid, jnp.int32), lot, side="right")
    return jax.random.permutation(jax.random.fold_in(key, 2), number_of)[grade].astype(jnp.int32)


def gaussian(rng, extent, deviation, bound, shards=(), kind=jnp.bfloat16):
    values = deviation * jax.random.normal(rng, extent, jnp.float32)
    if shards:
        values = values * levels(rng, extent, shards, -0.22, 0.18)
    return jnp.clip(values, -bound, bound).astype(kind)


def setup_inputs(seed: int = 0) -> dict:
    splits = jax.random.split(jax.random.key(seed), 8)
    latents = gaussian(splits[0], (PAIRS, 2, TOKENS, MODEL_WIDTH), 1.0, 6.0, ((0, 8), (2, 4)))
    targets = gaussian(splits[1], (PAIRS, 2, TOKENS, MODEL_WIDTH), 1.0, 6.0, ((0, 8), (2, 4)))
    frozen_weight = gaussian(splits[2], (MODEL_WIDTH, MODEL_WIDTH), MODEL_WIDTH ** -0.5, 0.125, ((0, 4),))
    adapter_down = gaussian(splits[3], (HARM_CLASSES, ADAPTER_RANK, MODEL_WIDTH), MODEL_WIDTH ** -0.5, 0.125, ((2, 8),))
    adapter_up = gaussian(splits[4], (HARM_CLASSES, ADAPTER_RANK, MODEL_WIDTH), ADAPTER_RANK ** -0.5, 0.75, ((2, 8),))
    categories = set_ends(ranked_ids(splits[5], (PAIRS,), HARM_CLASSES, 2), jax.random.fold_in(splits[5], 3), 0, HARM_CLASSES - 1).astype(jnp.int32)
    timesteps = set_ends(jax.random.randint(splits[6], (PAIRS,), 0, 1000), jax.random.fold_in(splits[6], 1), 0, 999).astype(jnp.int32)
    return dict(latents=latents, targets=targets, frozen_weight=frozen_weight, adapter_down=adapter_down, adapter_up=adapter_up, categories=categories, timesteps=timesteps)


ADAPTER_SCALE = 0.5
BETA = 1.0
LOSS_SCALE = 64.0


def single_pair(packed_group, frozen_weight, adapter_down, adapter_up):
    sample_in, sample_tgt, harm_class = packed_group
    selected_down = lax.dynamic_index_in_dim(adapter_down, harm_class.astype(jnp.int32), 0, keepdims=False)
    selected_up = lax.dynamic_index_in_dim(adapter_up, harm_class.astype(jnp.int32), 0, keepdims=False)
    flat_in = sample_in.reshape(2 * TOKENS, MODEL_WIDTH)
    base_out = jnp.dot(flat_in, frozen_weight, preferred_element_type=jnp.float32).reshape(2, TOKENS, MODEL_WIDTH)
    hidden_state = jnp.einsum("td,rd->tr", flat_in.astype(jnp.float32), selected_down.astype(jnp.float32)).astype(jnp.bfloat16)
    weight_change = ADAPTER_SCALE * jnp.einsum("lb,bz->lz", hidden_state.astype(jnp.float32), selected_up.astype(jnp.float32))
    weight_change = weight_change.reshape(2, TOKENS, MODEL_WIDTH)
    resid = base_out - sample_tgt.astype(jnp.float32)
    errdiff = jnp.sum(weight_change * (2.0 * resid + weight_change), axis=(1, 2)) / TOKENS
    update = (resid + weight_change).astype(jnp.bfloat16)
    hidden_k = hidden_state.reshape(2, TOKENS, ADAPTER_RANK)
    up_gradient_k = jnp.einsum("ktr,ktd->krd", hidden_k.astype(jnp.float32), update.astype(jnp.float32))
    back = jnp.einsum("ktd,rd->ktr", update.astype(jnp.float32), selected_up.astype(jnp.float32)).astype(jnp.bfloat16)
    down_gradient_k = jnp.einsum("ktr,ktd->krd", back.astype(jnp.float32), sample_in.astype(jnp.float32))
    return errdiff, up_gradient_k, down_gradient_k


def reference(latents, targets, frozen_weight, adapter_down, adapter_up, categories, timesteps):
    onehot = (categories[:, None] == jnp.arange(HARM_CLASSES, dtype=jnp.int32)[None, :]).astype(jnp.float32)
    counts = jnp.sum(onehot, axis=0)
    errdiff, up_gradient_k, down_gradient_k = lax.map(
        lambda packed_group: single_pair(packed_group, frozen_weight, adapter_down, adapter_up), (latents, targets, categories))
    kappa = BETA * (0.5 + timesteps.astype(jnp.float32) / 1000.0)
    zvalue = kappa * (errdiff[:, 0] - errdiff[:, 1])
    losses = jax.nn.softplus(zvalue)
    pair_total = jnp.sum(onehot * counts[None, :], axis=1)
    coef_pair = LOSS_SCALE * kappa * jax.nn.sigmoid(zvalue) / pair_total
    signs = jnp.array([2.0, -2.0], dtype=jnp.float32)
    coefficient = coef_pair[:, None] * signs[None, :] / TOKENS
    pairwise_up = ADAPTER_SCALE * jnp.sum(coefficient[:, :, None, None] * up_gradient_k, axis=1)
    pairwise_down = ADAPTER_SCALE * jnp.sum(coefficient[:, :, None, None] * down_gradient_k, axis=1)
    grad_up = jax.ops.segment_sum(pairwise_up, categories, num_segments=HARM_CLASSES)
    grad_down = jax.ops.segment_sum(pairwise_down, categories, num_segments=HARM_CLASSES)
    return grad_down, grad_up, losses
```

```python
import jax
import jax.numpy as jnp
from jax import lax
from jax.sharding import PartitionSpec as P

ADAPTER_SCALE = 0.5
BETA = 1.0
LOSS_SCALE = 64.0
F32 = jnp.float32
BF16 = jnp.bfloat16


def dot(a, b, ca, cb):
    return lax.dot_general(a, b, (((ca,), (cb,)), ((), ())), preferred_element_type=F32)


def local(latents, targets, frozen_weight, adapter_down, adapter_up, categories, timesteps):
    _, _, rows, feat = latents.shape
    classes, rank, cols = adapter_down.shape
    dp = lax.axis_size("dp")
    fs = lax.axis_size("fsdp")
    tokens = rows * fs
    cats = lax.all_gather(categories, "dp", axis=0, tiled=True)
    both = jnp.concatenate([adapter_down, adapter_up], axis=1)
    chosen = jnp.take(both, cats, axis=0)
    got = lax.all_to_all(chosen, "dp", split_axis=0, concat_axis=0, tiled=True)
    full = got.transpose(1, 0, 2).reshape(2 * rank, feat)
    down, up = full[:rank], full[rank:]
    x = latents.reshape(2 * rows, feat)
    t = targets.reshape(2 * rows, feat)
    sign = jnp.where(jnp.arange(2 * rows) < rows, 1.0, -1.0).astype(F32)[:, None]
    vz_exact = dot(up, frozen_weight, 1, 1)
    vz = vz_exact.astype(BF16)
    v = lax.all_gather(vz, "fsdp", axis=1, tiled=True)
    h = dot(x, down, 1, 1).astype(BF16)
    hs = h * sign.astype(BF16)
    g = dot(hs, x, 0, 0).astype(BF16)
    gz = lax.all_to_all(g.reshape(rank, fs, feat // fs), "fsdp", split_axis=1, concat_axis=1, tiled=True)
    gz_wide = jnp.sum(gz.astype(F32), axis=1)
    gz = gz_wide.astype(BF16)
    uu = dot(up, up, 1, 1)
    huu = ADAPTER_SCALE * lax.dot(h.astype(F32), uu, precision=lax.Precision.HIGHEST)
    s = dot(x, v, 1, 1) - dot(t, up, 1, 1) + huu
    err = jnp.sum(sign * (ADAPTER_SCALE * h.astype(F32) * (2.0 * s - huu)))
    err = err + 2.0 * ADAPTER_SCALE * jnp.sum(gz_wide * (vz_exact - vz.astype(F32)))
    diff = lax.psum(err, "fsdp") / tokens
    kappa = BETA * (0.5 + timesteps.astype(F32) / 1000.0)
    z = kappa * diff
    losses = jax.nn.softplus(z)
    total = jnp.sum((cats == categories[0]).astype(F32))
    scale = ADAPTER_SCALE * LOSS_SCALE * kappa * jax.nn.sigmoid(z) / total * 2.0 / tokens
    back = (s * sign).astype(BF16)
    pd = dot(back, x, 0, 0)
    m = dot(hs, h, 0, 0)
    pu = dot(gz, frozen_weight, 1, 0) - dot(hs, t, 0, 0) + ADAPTER_SCALE * dot(m, up.astype(F32), 1, 0)
    both = (jnp.concatenate([pd, pu], axis=0) * scale[0]).astype(BF16)
    pieces = both.reshape(2, fs, rank // fs, dp, cols).transpose(1, 3, 0, 2, 4)
    pieces = lax.all_to_all(pieces, "fsdp", split_axis=0, concat_axis=0, tiled=True)
    pieces = jnp.sum(pieces.astype(F32), axis=0).astype(BF16)
    pieces = lax.all_to_all(pieces, "dp", split_axis=0, concat_axis=0, tiled=True)
    onehot = (cats[:, None] == jnp.arange(classes, dtype=jnp.int32)[None, :]).astype(BF16)
    out = jnp.einsum("pc,pkrd->ckrd", onehot, pieces, preferred_element_type=F32).astype(BF16)
    out = lax.all_gather(out, "fsdp", axis=2, tiled=True).astype(F32)
    return out[:, 0], out[:, 1], losses


def solution(mesh):
    placed = (
        P("dp", None, "fsdp", None),
        P("dp", None, "fsdp", None),
        P("fsdp", None),
        P(None, None, "dp"),
        P(None, None, "dp"),
        P("dp"),
        P("dp"),
    )
    return jax.shard_map(
        local,
        mesh=mesh,
        in_specs=placed,
        out_specs=(P(None, None, "dp"), P(None, None, "dp"), P("dp")),
        check_vma=False,
    )
```

```python
import functools

import jax
import jax.numpy as jnp
from jax import lax
from jax.experimental import pallas as pl
from jax.experimental.pallas import tpu as pltpu
from jax.sharding import PartitionSpec as P

ADAPTER_SCALE = 0.5
BETA = 1.0
LOSS_SCALE = 64.0
F32 = jnp.float32
BF16 = jnp.bfloat16
MESH = pl.DeviceIdType.MESH


def dot(a, b, cb):
    return lax.dot_general(a, b, (((1,), (cb,)), ((), ())), preferred_element_type=F32)


def halves(a):
    high = a.astype(BF16)
    return high, (a - high.astype(F32)).astype(BF16)


def kernel(dp, fs, meta, x, t, w, ad, au, gd, gu, loss,
           meta_all, us, ur, ds, dr, up, down, vr, vt, gs, gr, er, ps, pr, acc, orr,
           ms_s, ms_r, u_s, u_r, d_s, d_r, v_s, v_r, g_s, g_r, e_s, e_r, p_s, p_r, o_s, o_r):
    classes, rank, cols = ad.shape
    both_rows, feat = x.shape
    rows = both_rows // 2
    fz = feat // fs
    tokens = rows * fs
    hr = rank // 2
    rz = rank // fs
    n = dp * fs
    md, mz = lax.axis_index("dp"), lax.axis_index("fsdp")
    me = md * fs + mz

    def remote(src, dst, ss, rs, d, z):
        return pltpu.make_async_remote_copy(
            src_ref=src, dst_ref=dst, send_sem=ss, recv_sem=rs, device_id=(d, z), device_id_type=MESH)

    def each(count, body):
        def step(i, carry):
            body(i)
            return carry
        lax.fori_loop(1, count, step, 0)

    def peer_d(i):
        return lax.rem(md + i, dp)

    def peer_z(i):
        return lax.rem(mz + i, fs)

    def peer_n(i):
        lin = lax.rem(me + i, n)
        return lin // fs, lax.rem(lin, fs)

    barrier = pltpu.get_barrier_semaphore()

    def greet(i):
        d, z = peer_n(i)
        pl.semaphore_signal(barrier, inc=1, device_id=(d, z), device_id_type=MESH)

    each(n, greet)
    pl.semaphore_wait(barrier, n - 1)

    meta_all[md] = meta[...]
    each(dp, lambda i: remote(meta, meta_all.at[md], ms_s.at[i], ms_r.at[md], peer_d(i), mz).start())

    def meta_wait(i):
        d = peer_d(i)
        remote(meta, meta_all.at[d], ms_s.at[i], ms_r.at[d], d, mz).wait_recv()

    each(dp, meta_wait)

    def pick(source, d):
        cat = meta_all[d, 0:1, 0:1]
        out = jnp.zeros((rank, cols), F32)
        for c in range(classes):
            out = out + (cat == c).astype(F32) * source[c].astype(F32)
        return jnp.concatenate([out[:hr], out[hr:]], axis=1).astype(BF16)

    def send_part(source, sent, got, ss, rs):
        def body(i):
            d = peer_d(i)
            sent[d] = pick(source, d)
            remote(sent.at[d], got.at[md], ss.at[i], rs.at[md], d, mz).start()
        each(dp, body)
        got[md] = pick(source, md)

    send_part(au, us, ur, u_s, u_r)
    send_part(ad, ds, dr, d_s, d_r)

    def take_part(sent, got, ss, rs, whole):
        def body(i):
            d = peer_d(i)
            remote(sent.at[d], got.at[d], ss.at[i], rs.at[d], d, mz).wait_recv()
        each(dp, body)
        for d in range(dp):
            piece = got[d].astype(F32)
            whole[0:hr, cols * d:cols * (d + 1)] = piece[:, :cols].astype(BF16)
            whole[hr:rank, cols * d:cols * (d + 1)] = piece[:, cols:].astype(BF16)

    take_part(us, ur, u_s, u_r, up)
    v_exact = dot(up[...], w[...], 1)
    v_half = v_exact.astype(BF16)
    vr[mz] = v_half
    each(fs, lambda i: remote(vr.at[mz], vr.at[mz], v_s.at[i], v_r.at[mz], md, peer_z(i)).start())

    take_part(ds, dr, d_s, d_r, down)
    ht = dot(down[...], x[...], 1).astype(BF16)
    sign = jnp.where(lax.broadcasted_iota(jnp.int32, (1, 2 * rows), 1) < rows, 1.0, -1.0).astype(F32)
    hf = ht.astype(F32)
    hts = (hf * sign).astype(BF16)
    g = dot(hts, x[...], 0)
    for z in range(fs):
        gs[z] = g[:, fz * z:fz * (z + 1)].astype(BF16)
    each(fs, lambda i: remote(gs.at[peer_z(i)], gr.at[mz], g_s.at[i], g_r.at[mz], md, peer_z(i)).start())
    gr[mz] = gs[mz]

    uu_h, uu_l = halves(dot(up[...], up[...], 1))
    huu = ADAPTER_SCALE * (dot(uu_h, ht, 0) + dot(uu_l, ht, 0))
    st = huu - dot(up[...], t[...], 1)
    m_h, m_l = halves(ADAPTER_SCALE * dot(hts, ht, 1))
    pu = dot(m_h, up[...], 0) + dot(m_l, up[...], 0) - dot(hts, t[...], 0)

    def v_wait(i):
        z = peer_z(i)
        remote(vr.at[z], vr.at[z], v_s.at[i], v_r.at[z], md, z).wait_recv()

    each(fs, v_wait)
    for z in range(fs):
        vt[:, fz * z:fz * (z + 1)] = vr[z]
    st = st + dot(vt[...], x[...], 1)

    def g_wait(i):
        z = peer_z(i)
        remote(gs.at[z], gr.at[z], g_s.at[i], g_r.at[z], md, z).wait_recv()

    each(fs, g_wait)
    g_wide = gr[0].astype(F32)
    for z in range(1, fs):
        g_wide = g_wide + gr[z].astype(F32)
    err = jnp.sum(sign * (ADAPTER_SCALE * hf * (2.0 * st - huu)), axis=(0, 1), keepdims=True)
    err = err + 2.0 * ADAPTER_SCALE * jnp.sum(
        g_wide * (v_exact - v_half.astype(F32)), axis=(0, 1), keepdims=True)
    er[mz] = jnp.broadcast_to(err, (8, 128))
    each(fs, lambda i: remote(er.at[mz], er.at[mz], e_s.at[i], e_r.at[mz], md, peer_z(i)).start())

    back = (st * sign).astype(BF16)
    pd = dot(back, x[...], 0)
    g_h, g_l = halves(g_wide)
    pu = pu + dot(g_h, w[...], 0) + dot(g_l, w[...], 0)

    def e_wait(i):
        z = peer_z(i)
        remote(er.at[z], er.at[z], e_s.at[i], e_r.at[z], md, z).wait_recv()

    each(fs, e_wait)
    diff = er[0]
    for z in range(1, fs):
        diff = diff + er[z]
    diff = diff[0:1, :] / tokens
    my_cat = meta[0:1, :]
    kappa = BETA * (0.5 + meta[1:2, :].astype(F32) / 1000.0)
    zvalue = kappa * diff
    decay = jnp.exp(-jnp.abs(zvalue))
    loss[...] = jnp.broadcast_to(jnp.maximum(zvalue, 0.0) + jnp.log1p(decay), (8, 128))
    total = lax.fori_loop(
        0, dp, lambda d, s: s + (meta_all[d, 0:1, :] == my_cat).astype(F32), jnp.zeros((1, 128), F32))
    sigmoid = jnp.where(zvalue >= 0.0, 1.0, decay) / (1.0 + decay)
    scale = (ADAPTER_SCALE * 2.0 * LOSS_SCALE / tokens) * kappa * sigmoid / total
    pd = pd * scale[:, 0:1]
    pu = pu * scale[:, 0:1]

    for d in range(dp):
        joined = jnp.concatenate(
            [pd[:, cols * d:cols * (d + 1)], pu[:, cols * d:cols * (d + 1)]], axis=1).astype(BF16)
        for z in range(fs):
            ps[z, d] = joined[rz * z:rz * (z + 1)]

    def p_send(i):
        d, z = peer_n(i)
        remote(ps.at[z, d], pr.at[mz, md], p_s.at[z, d], p_r.at[mz, md], d, z).start()

    def p_wait(i):
        d, z = peer_n(i)
        remote(ps.at[z, d], pr.at[z, d], p_s.at[z, d], p_r.at[z, d], d, z).wait_recv()

    each(n, p_send)
    pr[mz, md] = ps[mz, md]
    acc[...] = jnp.zeros_like(acc)
    each(n, p_wait)

    def gather(d, carry):
        piece = pr[0, d].astype(F32)
        for z in range(1, fs):
            piece = piece + pr[z, d].astype(F32)
        cat = meta_all[d, 0:1, 0:1]
        for c in range(classes):
            acc[c] += (cat == c).astype(F32) * piece
        return carry

    lax.fori_loop(0, dp, gather, 0)
    orr[mz] = acc[...].astype(BF16)
    each(fs, lambda i: remote(orr.at[mz], orr.at[mz], o_s.at[i], o_r.at[mz], md, peer_z(i)).start())

    def o_wait(i):
        z = peer_z(i)
        remote(orr.at[z], orr.at[z], o_s.at[i], o_r.at[z], md, z).wait_recv()

    each(fs, o_wait)
    for z in range(fs):
        part = orr[z].astype(F32)
        gd[:, rz * z:rz * (z + 1), :] = part[:, :, :cols]
        gu[:, rz * z:rz * (z + 1), :] = part[:, :, cols:]

    def sent_d(i):
        d = peer_d(i)
        remote(meta, meta_all.at[md], ms_s.at[i], ms_r.at[md], d, mz).wait_send()
        remote(us.at[d], ur.at[md], u_s.at[i], u_r.at[md], d, mz).wait_send()
        remote(ds.at[d], dr.at[md], d_s.at[i], d_r.at[md], d, mz).wait_send()

    def sent_z(i):
        z = peer_z(i)
        remote(vr.at[mz], vr.at[mz], v_s.at[i], v_r.at[mz], md, z).wait_send()
        remote(gs.at[z], gr.at[mz], g_s.at[i], g_r.at[mz], md, z).wait_send()
        remote(er.at[mz], er.at[mz], e_s.at[i], e_r.at[mz], md, z).wait_send()
        remote(orr.at[mz], orr.at[mz], o_s.at[i], o_r.at[mz], md, z).wait_send()

    def sent_n(i):
        d, z = peer_n(i)
        remote(ps.at[z, d], pr.at[mz, md], p_s.at[z, d], p_r.at[mz, md], d, z).wait_send()

    each(dp, sent_d)
    each(fs, sent_z)
    each(n, sent_n)


def local(dp, fs, latents, targets, frozen_weight, adapter_down, adapter_up, categories, timesteps):
    _, _, rows, feat = latents.shape
    classes, rank, cols = adapter_down.shape
    fz = feat // fs
    hr, rz = rank // 2, rank // fs
    meta = jnp.concatenate([
        jnp.broadcast_to(categories[:, None], (1, 128)),
        jnp.broadcast_to(timesteps[:, None], (7, 128))], axis=0)
    vm = pl.BlockSpec(memory_space=pltpu.VMEM)
    dma = pltpu.SemaphoreType.DMA
    out = jax.ShapeDtypeStruct((classes, rank, cols), F32)
    gd, gu, loss = pl.pallas_call(
        functools.partial(kernel, dp, fs),
        out_shape=(out, out, jax.ShapeDtypeStruct((8, 128), F32)),
        in_specs=[vm] * 6,
        out_specs=(vm,) * 3,
        scratch_shapes=[
            pltpu.VMEM((dp, 8, 128), jnp.int32),
            pltpu.VMEM((dp, hr, 2 * cols), BF16),
            pltpu.VMEM((dp, hr, 2 * cols), BF16),
            pltpu.VMEM((dp, hr, 2 * cols), BF16),
            pltpu.VMEM((dp, hr, 2 * cols), BF16),
            pltpu.VMEM((rank, feat), BF16),
            pltpu.VMEM((rank, feat), BF16),
            pltpu.VMEM((fs, rank, fz), BF16),
            pltpu.VMEM((rank, feat), BF16),
            pltpu.VMEM((fs, rank, fz), BF16),
            pltpu.VMEM((fs, rank, fz), BF16),
            pltpu.VMEM((fs, 8, 128), F32),
            pltpu.VMEM((fs, dp, rz, 2 * cols), BF16),
            pltpu.VMEM((fs, dp, rz, 2 * cols), BF16),
            pltpu.VMEM((classes, rz, 2 * cols), F32),
            pltpu.VMEM((fs, classes, rz, 2 * cols), BF16),
            dma((dp,)), dma((dp,)), dma((dp,)), dma((dp,)), dma((dp,)), dma((dp,)),
            dma((fs,)), dma((fs,)), dma((fs,)), dma((fs,)), dma((fs,)), dma((fs,)),
            dma((fs, dp)), dma((fs, dp)), dma((fs,)), dma((fs,)),
        ],
        compiler_params=pltpu.CompilerParams(
            collective_id=0, has_side_effects=True, vmem_limit_bytes=48 * 1024 * 1024),
    )(meta, latents.reshape(2 * rows, feat), targets.reshape(2 * rows, feat),
      frozen_weight, adapter_down, adapter_up)
    return gd, gu, loss[0, 0:1]


def solution(mesh):
    placed = (
        P("dp", None, "fsdp", None),
        P("dp", None, "fsdp", None),
        P("fsdp", None),
        P(None, None, "dp"),
        P(None, None, "dp"),
        P("dp"),
        P("dp"),
    )
    return jax.shard_map(
        functools.partial(local, mesh.shape["dp"], mesh.shape["fsdp"]),
        mesh=mesh,
        in_specs=placed,
        out_specs=(P(None, None, "dp"), P(None, None, "dp"), P("dp")),
        check_vma=False,
    )
```

```python
import functools

import jax
import jax.numpy as jnp
from jax import lax
from jax.experimental import pallas as pl
from jax.experimental.pallas import tpu as pltpu
from jax.sharding import PartitionSpec as P

ADAPTER_SCALE = 0.5
BETA = 1.0
LOSS_SCALE = 64.0
F32 = jnp.float32
BF16 = jnp.bfloat16
MESH = pl.DeviceIdType.MESH


def dot(a, b, cb):
    return lax.dot_general(a, b, (((1,), (cb,)), ((), ())), preferred_element_type=F32)


def halves(a):
    high = a.astype(BF16)
    return high, (a - high.astype(F32)).astype(BF16)


def kernel(dp, fs, meta, x_in, t_in, w_in, ad_in, au_in, gd, gu, loss,
           x, t, w, ad, au, in_sem, meta_all, us, ur, ds, dr, up, down, vr, vt, gs, gr, er, ps, pr, acc, orr,
           ms_s, ms_r, u_s, u_r, d_s, d_r, v_s, v_r, g_s, g_r, e_s, e_r, p_s, p_r, o_s, o_r):
    classes, rank, cols = ad.shape
    both_rows, feat = x.shape
    rows = both_rows // 2
    fz = feat // fs
    tokens = rows * fs
    hr = rank // 2
    rz = rank // fs
    n = dp * fs
    md, mz = lax.axis_index("dp"), lax.axis_index("fsdp")
    me = md * fs + mz

    def remote(src, dst, ss, rs, d, z):
        return pltpu.make_async_remote_copy(
            src_ref=src, dst_ref=dst, send_sem=ss, recv_sem=rs, device_id=(d, z), device_id_type=MESH)

    def each(count, body):
        def step(i, carry):
            body(i)
            return carry
        lax.fori_loop(1, count, step, 0)

    def peer_d(i):
        return lax.rem(md + i, dp)

    def peer_z(i):
        return lax.rem(mz + i, fs)

    def peer_n(i):
        lin = lax.rem(me + i, n)
        return lin // fs, lax.rem(lin, fs)

    loads = [pltpu.make_async_copy(src, dst, in_sem.at[i]) for i, (src, dst) in enumerate(
        ((au_in, au), (ad_in, ad), (w_in, w), (x_in, x), (t_in, t)))]
    for load in loads:
        load.start()

    barrier = pltpu.get_barrier_semaphore()

    def greet(i):
        d, z = peer_n(i)
        pl.semaphore_signal(barrier, inc=1, device_id=(d, z), device_id_type=MESH)

    each(n, greet)
    pl.semaphore_wait(barrier, n - 1)

    meta_all[md] = meta[...]
    each(dp, lambda i: remote(meta, meta_all.at[md], ms_s.at[i], ms_r.at[md], peer_d(i), mz).start())

    def meta_wait(i):
        d = peer_d(i)
        remote(meta, meta_all.at[d], ms_s.at[i], ms_r.at[d], d, mz).wait_recv()

    each(dp, meta_wait)

    def pick(source, d):
        cat = meta_all[d, 0:1, 0:1]
        out = jnp.zeros((rank, cols), F32)
        for c in range(classes):
            out = out + (cat == c).astype(F32) * source[c].astype(F32)
        return jnp.concatenate([out[:hr], out[hr:]], axis=1).astype(BF16)

    def send_part(source, sent, got, ss, rs):
        def body(i):
            d = peer_d(i)
            sent[d] = pick(source, d)
            remote(sent.at[d], got.at[md], ss.at[i], rs.at[md], d, mz).start()
        each(dp, body)
        got[md] = pick(source, md)

    loads[0].wait()
    send_part(au, us, ur, u_s, u_r)
    loads[1].wait()
    send_part(ad, ds, dr, d_s, d_r)

    def take_part(sent, got, ss, rs, whole):
        def body(i):
            d = peer_d(i)
            remote(sent.at[d], got.at[d], ss.at[i], rs.at[d], d, mz).wait_recv()
        each(dp, body)
        for d in range(dp):
            piece = got[d].astype(F32)
            whole[0:hr, cols * d:cols * (d + 1)] = piece[:, :cols].astype(BF16)
            whole[hr:rank, cols * d:cols * (d + 1)] = piece[:, cols:].astype(BF16)

    for load in loads[2:]:
        load.wait()
    take_part(us, ur, u_s, u_r, up)
    v_exact = dot(w[...], up[...], 1).T
    v_half = v_exact.astype(BF16)
    vr[mz] = v_half
    each(fs, lambda i: remote(vr.at[mz], vr.at[mz], v_s.at[i], v_r.at[mz], md, peer_z(i)).start())

    take_part(ds, dr, d_s, d_r, down)
    ht = dot(down[...], x[...], 1).astype(BF16)
    sign = jnp.where(lax.broadcasted_iota(jnp.int32, (1, 2 * rows), 1) < rows, 1.0, -1.0).astype(F32)
    hf = ht.astype(F32)
    hts = (hf * sign).astype(BF16)
    g = dot(hts, x[...], 0)
    for z in range(fs):
        gs[z] = g[:, fz * z:fz * (z + 1)].astype(BF16)
    each(fs, lambda i: remote(gs.at[peer_z(i)], gr.at[mz], g_s.at[i], g_r.at[mz], md, peer_z(i)).start())
    gr[mz] = gs[mz]

    uu_h, uu_l = halves(dot(up[...], up[...], 1))
    huu = ADAPTER_SCALE * (dot(uu_h, ht, 0) + dot(uu_l, ht, 0))
    st = huu - dot(up[...], t[...], 1)
    m_h, m_l = halves(ADAPTER_SCALE * dot(hts, ht, 1))
    pu = dot(m_h, up[...], 0) + dot(m_l, up[...], 0) - dot(hts, t[...], 0)

    def v_wait(i):
        z = peer_z(i)
        remote(vr.at[z], vr.at[z], v_s.at[i], v_r.at[z], md, z).wait_recv()

    each(fs, v_wait)
    for z in range(fs):
        vt[:, fz * z:fz * (z + 1)] = vr[z]
    st = st + dot(vt[...], x[...], 1)
    back = (st * sign).astype(BF16)
    pd = dot(back, x[...], 0)

    def g_wait(i):
        z = peer_z(i)
        remote(gs.at[z], gr.at[z], g_s.at[i], g_r.at[z], md, z).wait_recv()

    each(fs, g_wait)
    g_wide = gr[0].astype(F32)
    for z in range(1, fs):
        g_wide = g_wide + gr[z].astype(F32)
    err = jnp.sum(sign * (ADAPTER_SCALE * hf * (2.0 * st - huu)), axis=(0, 1), keepdims=True)
    err = err + 2.0 * ADAPTER_SCALE * jnp.sum(
        g_wide * (v_exact - v_half.astype(F32)), axis=(0, 1), keepdims=True)
    er[mz] = jnp.broadcast_to(err, (8, 128))
    each(fs, lambda i: remote(er.at[mz], er.at[mz], e_s.at[i], e_r.at[mz], md, peer_z(i)).start())

    g_h, g_l = halves(g_wide)
    pu = pu + dot(g_h, w[...], 0) + dot(g_l, w[...], 0)

    def e_wait(i):
        z = peer_z(i)
        remote(er.at[z], er.at[z], e_s.at[i], e_r.at[z], md, z).wait_recv()

    each(fs, e_wait)
    diff = er[0]
    for z in range(1, fs):
        diff = diff + er[z]
    diff = diff[0:1, :] / tokens
    my_cat = meta[0:1, :]
    kappa = BETA * (0.5 + meta[1:2, :].astype(F32) / 1000.0)
    zvalue = kappa * diff
    decay = jnp.exp(-jnp.abs(zvalue))
    loss[...] = jnp.broadcast_to(jnp.maximum(zvalue, 0.0) + jnp.log1p(decay), (8, 128))
    total = lax.fori_loop(
        0, dp, lambda d, s: s + (meta_all[d, 0:1, :] == my_cat).astype(F32), jnp.zeros((1, 128), F32))
    sigmoid = jnp.where(zvalue >= 0.0, 1.0, decay) / (1.0 + decay)
    scale = (ADAPTER_SCALE * 2.0 * LOSS_SCALE / tokens) * kappa * sigmoid / total
    pd = pd * scale[:, 0:1]
    pu = pu * scale[:, 0:1]

    for d in range(dp):
        joined = jnp.concatenate(
            [pd[:, cols * d:cols * (d + 1)], pu[:, cols * d:cols * (d + 1)]], axis=1).astype(BF16)
        for z in range(fs):
            ps[z, d] = joined[rz * z:rz * (z + 1)]

    def p_send(i):
        d, z = peer_n(i)
        remote(ps.at[z, d], pr.at[mz, md], p_s.at[z, d], p_r.at[mz, md], d, z).start()

    def p_wait(i):
        d, z = peer_n(i)
        remote(ps.at[z, d], pr.at[z, d], p_s.at[z, d], p_r.at[z, d], d, z).wait_recv()

    each(n, p_send)
    pr[mz, md] = ps[mz, md]
    acc[...] = jnp.zeros_like(acc)
    each(n, p_wait)

    def gather(d, carry):
        piece = pr[0, d].astype(F32)
        for z in range(1, fs):
            piece = piece + pr[z, d].astype(F32)
        cat = meta_all[d, 0:1, 0:1]
        for c in range(classes):
            acc[c] += (cat == c).astype(F32) * piece
        return carry

    lax.fori_loop(0, dp, gather, 0)
    orr[mz] = acc[...].astype(BF16)
    each(fs, lambda i: remote(orr.at[mz], orr.at[mz], o_s.at[i], o_r.at[mz], md, peer_z(i)).start())

    def o_wait(i):
        z = peer_z(i)
        remote(orr.at[z], orr.at[z], o_s.at[i], o_r.at[z], md, z).wait_recv()

    each(fs, o_wait)
    for z in range(fs):
        part = orr[z].astype(F32)
        gd[:, rz * z:rz * (z + 1), :] = part[:, :, :cols]
        gu[:, rz * z:rz * (z + 1), :] = part[:, :, cols:]

    def sent_d(i):
        d = peer_d(i)
        remote(meta, meta_all.at[md], ms_s.at[i], ms_r.at[md], d, mz).wait_send()
        remote(us.at[d], ur.at[md], u_s.at[i], u_r.at[md], d, mz).wait_send()
        remote(ds.at[d], dr.at[md], d_s.at[i], d_r.at[md], d, mz).wait_send()

    def sent_z(i):
        z = peer_z(i)
        remote(vr.at[mz], vr.at[mz], v_s.at[i], v_r.at[mz], md, z).wait_send()
        remote(gs.at[z], gr.at[mz], g_s.at[i], g_r.at[mz], md, z).wait_send()
        remote(er.at[mz], er.at[mz], e_s.at[i], e_r.at[mz], md, z).wait_send()
        remote(orr.at[mz], orr.at[mz], o_s.at[i], o_r.at[mz], md, z).wait_send()

    def sent_n(i):
        d, z = peer_n(i)
        remote(ps.at[z, d], pr.at[mz, md], p_s.at[z, d], p_r.at[mz, md], d, z).wait_send()

    each(dp, sent_d)
    each(fs, sent_z)
    each(n, sent_n)


def local(dp, fs, latents, targets, frozen_weight, adapter_down, adapter_up, categories, timesteps):
    _, _, rows, feat = latents.shape
    classes, rank, cols = adapter_down.shape
    fz = feat // fs
    hr, rz = rank // 2, rank // fs
    meta = jnp.concatenate([
        jnp.broadcast_to(categories[:, None], (1, 128)),
        jnp.broadcast_to(timesteps[:, None], (7, 128))], axis=0)
    vm = pl.BlockSpec(memory_space=pltpu.VMEM)
    dma = pltpu.SemaphoreType.DMA
    out = jax.ShapeDtypeStruct((classes, rank, cols), F32)
    gd, gu, loss = pl.pallas_call(
        functools.partial(kernel, dp, fs),
        out_shape=(out, out, jax.ShapeDtypeStruct((8, 128), F32)),
        in_specs=[vm] + [pl.BlockSpec(memory_space=pl.ANY)] * 5,
        out_specs=(vm,) * 3,
        scratch_shapes=[
            pltpu.VMEM((2 * rows, feat), BF16),
            pltpu.VMEM((2 * rows, feat), BF16),
            pltpu.VMEM((fz, feat), BF16),
            pltpu.VMEM((classes, rank, cols), BF16),
            pltpu.VMEM((classes, rank, cols), BF16),
            dma((5,)),
            pltpu.VMEM((dp, 8, 128), jnp.int32),
            pltpu.VMEM((dp, hr, 2 * cols), BF16),
            pltpu.VMEM((dp, hr, 2 * cols), BF16),
            pltpu.VMEM((dp, hr, 2 * cols), BF16),
            pltpu.VMEM((dp, hr, 2 * cols), BF16),
            pltpu.VMEM((rank, feat), BF16),
            pltpu.VMEM((rank, feat), BF16),
            pltpu.VMEM((fs, rank, fz), BF16),
            pltpu.VMEM((rank, feat), BF16),
            pltpu.VMEM((fs, rank, fz), BF16),
            pltpu.VMEM((fs, rank, fz), BF16),
            pltpu.VMEM((fs, 8, 128), F32),
            pltpu.VMEM((fs, dp, rz, 2 * cols), BF16),
            pltpu.VMEM((fs, dp, rz, 2 * cols), BF16),
            pltpu.VMEM((classes, rz, 2 * cols), F32),
            pltpu.VMEM((fs, classes, rz, 2 * cols), BF16),
            dma((dp,)), dma((dp,)), dma((dp,)), dma((dp,)), dma((dp,)), dma((dp,)),
            dma((fs,)), dma((fs,)), dma((fs,)), dma((fs,)), dma((fs,)), dma((fs,)),
            dma((fs, dp)), dma((fs, dp)), dma((fs,)), dma((fs,)),
        ],
        compiler_params=pltpu.CompilerParams(
            collective_id=0, has_side_effects=True, vmem_limit_bytes=56 * 1024 * 1024),
    )(meta, latents.reshape(2 * rows, feat), targets.reshape(2 * rows, feat),
      frozen_weight, adapter_down, adapter_up)
    return gd, gu, loss[0, 0:1]


def solution(mesh):
    placed = (
        P("dp", None, "fsdp", None),
        P("dp", None, "fsdp", None),
        P("fsdp", None),
        P(None, None, "dp"),
        P(None, None, "dp"),
        P("dp"),
        P("dp"),
    )
    return jax.shard_map(
        functools.partial(local, mesh.shape["dp"], mesh.shape["fsdp"]),
        mesh=mesh,
        in_specs=placed,
        out_specs=(P(None, None, "dp"), P(None, None, "dp"), P("dp")),
        check_vma=False,
    )
```

```python
import functools

import jax
import jax.numpy as jnp
from jax import lax
from jax.experimental import pallas as pl
from jax.experimental.pallas import tpu as pltpu
from jax.sharding import PartitionSpec as P

ADAPTER_SCALE = 0.5
BETA = 1.0
LOSS_SCALE = 64.0
F32 = jnp.float32
BF16 = jnp.bfloat16
MESH = pl.DeviceIdType.MESH


def dot(a, b, cb):
    return lax.dot_general(a, b, (((1,), (cb,)), ((), ())), preferred_element_type=F32)


def halves(a):
    high = a.astype(BF16)
    return high, (a - high.astype(F32)).astype(BF16)


def kernel(dp, fs, meta, x_in, t_in, w_in, ad_in, au_in, gd, gu, loss,
           x, t, w, ad, au, in_sem, pf, meta_all, us, ur, ds, dr, up, down, vr, vt, gs, gr, er, ps, pr, acc, orr,
           ms_s, ms_r, u_s, u_r, d_s, d_r, v_s, v_r, g_s, g_r, e_s, e_r, p_s, p_r, o_s, o_r):
    classes, rank, cols = ad.shape
    both_rows, feat = x.shape
    rows = both_rows // 2
    fz = feat // fs
    tokens = rows * fs
    hr = rank // 2
    rz = rank // fs
    n = dp * fs
    md, mz = lax.axis_index("dp"), lax.axis_index("fsdp")
    me = md * fs + mz

    def remote(src, dst, ss, rs, d, z):
        return pltpu.make_async_remote_copy(
            src_ref=src, dst_ref=dst, send_sem=ss, recv_sem=rs, device_id=(d, z), device_id_type=MESH)

    def each(count, body):
        def step(i, carry):
            body(i)
            return carry
        lax.fori_loop(1, count, step, 0)

    def peer_d(i):
        return lax.rem(md + i, dp)

    def peer_z(i):
        return lax.rem(mz + i, fs)

    def peer_n(i):
        lin = lax.rem(me + i, n)
        return lin // fs, lax.rem(lin, fs)

    loads = [pltpu.make_async_copy(src, dst, in_sem.at[i]) for i, (src, dst) in enumerate(
        ((au_in, au), (ad_in, ad), (w_in, w), (x_in, x), (t_in, t)))]
    for load in loads:
        load.start()

    barrier = pltpu.get_barrier_semaphore()

    def greet(i):
        d, z = peer_n(i)
        pl.semaphore_signal(barrier, inc=1, device_id=(d, z), device_id_type=MESH)

    each(n, greet)
    pl.semaphore_wait(barrier, n - 1)

    meta_all[md] = meta[...]
    each(dp, lambda i: remote(meta, meta_all.at[md], ms_s.at[i], ms_r.at[md], peer_d(i), mz).start())

    def meta_wait(i):
        d = peer_d(i)
        remote(meta, meta_all.at[d], ms_s.at[i], ms_r.at[d], d, mz).wait_recv()

    each(dp, meta_wait)

    def pick(source, d):
        cat = meta_all[d, 0:1, 0:1]
        out = jnp.zeros((rank, cols), F32)
        for c in range(classes):
            out = out + (cat == c).astype(F32) * source[c].astype(F32)
        return jnp.concatenate([out[:hr], out[hr:]], axis=1).astype(BF16)

    def send_part(source, sent, got, ss, rs):
        def body(i):
            d = peer_d(i)
            sent[d] = pick(source, d)
            remote(sent.at[d], got.at[md], ss.at[i], rs.at[md], d, mz).start()
        each(dp, body)
        got[md] = pick(source, md)

    loads[1].wait()
    send_part(ad, ds, dr, d_s, d_r)

    loads[0].wait()
    send_part(au, us, ur, u_s, u_r)

    def take_part(sent, got, ss, rs, whole):
        def body(i):
            d = peer_d(i)
            remote(sent.at[d], got.at[d], ss.at[i], rs.at[d], d, mz).wait_recv()
        each(dp, body)
        for d in range(dp):
            piece = got[d].astype(F32)
            whole[0:hr, cols * d:cols * (d + 1)] = piece[:, :cols].astype(BF16)
            whole[hr:rank, cols * d:cols * (d + 1)] = piece[:, cols:].astype(BF16)

    for load in loads[2:]:
        load.wait()
    take_part(ds, dr, d_s, d_r, down)
    ht = dot(down[...], x[...], 1).astype(BF16)
    sign = jnp.where(lax.broadcasted_iota(jnp.int32, (1, 2 * rows), 1) < rows, 1.0, -1.0).astype(F32)
    hf = ht.astype(F32)
    hts = (hf * sign).astype(BF16)
    g = dot(hts, x[...], 0)
    for z in range(fs):
        gs[z] = g[:, fz * z:fz * (z + 1)].astype(BF16)
    each(fs, lambda i: remote(gs.at[peer_z(i)], gr.at[mz], g_s.at[i], g_r.at[mz], md, peer_z(i)).start())
    gr[mz] = gs[mz]

    take_part(us, ur, u_s, u_r, up)
    v_exact = dot(w[...], up[...], 1).T
    v_half = v_exact.astype(BF16)
    vr[mz] = v_half
    each(fs, lambda i: remote(vr.at[mz], vr.at[mz], v_s.at[i], v_r.at[mz], md, peer_z(i)).start())

    uu_h, uu_l = halves(dot(up[...], up[...], 1))
    huu = ADAPTER_SCALE * (dot(uu_h, ht, 0) + dot(uu_l, ht, 0))
    st = huu - dot(up[...], t[...], 1)
    m_h, m_l = halves(ADAPTER_SCALE * dot(hts, ht, 1))
    pu = dot(m_h, up[...], 0) + dot(m_l, up[...], 0) - dot(hts, t[...], 0)

    def g_wait(i):
        z = peer_z(i)
        remote(gs.at[z], gr.at[z], g_s.at[i], g_r.at[z], md, z).wait_recv()

    each(fs, g_wait)
    g_wide = gr[0].astype(F32)
    for z in range(1, fs):
        g_wide = g_wide + gr[z].astype(F32)
    g_h, g_l = halves(g_wide)
    pu = pu + dot(g_h, w[...], 0) + dot(g_l, w[...], 0)

    def v_wait(i):
        z = peer_z(i)
        remote(vr.at[z], vr.at[z], v_s.at[i], v_r.at[z], md, z).wait_recv()

    each(fs, v_wait)
    for z in range(fs):
        vt[:, fz * z:fz * (z + 1)] = vr[z]
    st = st + dot(vt[...], x[...], 1)

    err = jnp.sum(sign * (ADAPTER_SCALE * hf * (2.0 * st - huu)), axis=(0, 1), keepdims=True)
    err = err + 2.0 * ADAPTER_SCALE * jnp.sum(
        g_wide * (v_exact - v_half.astype(F32)), axis=(0, 1), keepdims=True)
    er[mz] = jnp.broadcast_to(err, (8, 128))
    each(fs, lambda i: remote(er.at[mz], er.at[mz], e_s.at[i], e_r.at[mz], md, peer_z(i)).start())

    back = (st * sign).astype(BF16)
    pd = dot(back, x[...], 0)
    for d in range(dp):
        pf[d] = jnp.concatenate(
            [pd[:, cols * d:cols * (d + 1)], pu[:, cols * d:cols * (d + 1)]], axis=1)

    def e_wait(i):
        z = peer_z(i)
        remote(er.at[z], er.at[z], e_s.at[i], e_r.at[z], md, z).wait_recv()

    each(fs, e_wait)
    diff = er[0]
    for z in range(1, fs):
        diff = diff + er[z]
    diff = diff[0:1, :] / tokens
    my_cat = meta[0:1, :]
    kappa = BETA * (0.5 + meta[1:2, :].astype(F32) / 1000.0)
    zvalue = kappa * diff
    decay = jnp.exp(-jnp.abs(zvalue))
    loss[...] = jnp.broadcast_to(jnp.maximum(zvalue, 0.0) + jnp.log1p(decay), (8, 128))
    total = lax.fori_loop(
        0, dp, lambda d, s: s + (meta_all[d, 0:1, :] == my_cat).astype(F32), jnp.zeros((1, 128), F32))
    sigmoid = jnp.where(zvalue >= 0.0, 1.0, decay) / (1.0 + decay)
    scale = (ADAPTER_SCALE * 2.0 * LOSS_SCALE / tokens) * kappa * sigmoid / total

    for d in range(dp):
        joined = (pf[d] * scale[:, 0:1]).astype(BF16)
        for z in range(fs):
            ps[z, d] = joined[rz * z:rz * (z + 1)]

    def p_send(i):
        d, z = peer_n(i)
        remote(ps.at[z, d], pr.at[mz, md], p_s.at[z, d], p_r.at[mz, md], d, z).start()

    def p_wait(i):
        d, z = peer_n(i)
        remote(ps.at[z, d], pr.at[z, d], p_s.at[z, d], p_r.at[z, d], d, z).wait_recv()

    each(n, p_send)
    pr[mz, md] = ps[mz, md]
    acc[...] = jnp.zeros_like(acc)
    each(n, p_wait)

    def gather(d, carry):
        piece = pr[0, d].astype(F32)
        for z in range(1, fs):
            piece = piece + pr[z, d].astype(F32)
        cat = meta_all[d, 0:1, 0:1]
        for c in range(classes):
            acc[c] += (cat == c).astype(F32) * piece
        return carry

    lax.fori_loop(0, dp, gather, 0)
    orr[mz] = acc[...].astype(BF16)
    each(fs, lambda i: remote(orr.at[mz], orr.at[mz], o_s.at[i], o_r.at[mz], md, peer_z(i)).start())

    def o_wait(i):
        z = peer_z(i)
        remote(orr.at[z], orr.at[z], o_s.at[i], o_r.at[z], md, z).wait_recv()

    each(fs, o_wait)
    for z in range(fs):
        part = orr[z].astype(F32)
        gd[:, rz * z:rz * (z + 1), :] = part[:, :, :cols]
        gu[:, rz * z:rz * (z + 1), :] = part[:, :, cols:]

    def sent_d(i):
        d = peer_d(i)
        remote(meta, meta_all.at[md], ms_s.at[i], ms_r.at[md], d, mz).wait_send()
        remote(us.at[d], ur.at[md], u_s.at[i], u_r.at[md], d, mz).wait_send()
        remote(ds.at[d], dr.at[md], d_s.at[i], d_r.at[md], d, mz).wait_send()

    def sent_z(i):
        z = peer_z(i)
        remote(vr.at[mz], vr.at[mz], v_s.at[i], v_r.at[mz], md, z).wait_send()
        remote(gs.at[z], gr.at[mz], g_s.at[i], g_r.at[mz], md, z).wait_send()
        remote(er.at[mz], er.at[mz], e_s.at[i], e_r.at[mz], md, z).wait_send()
        remote(orr.at[mz], orr.at[mz], o_s.at[i], o_r.at[mz], md, z).wait_send()

    def sent_n(i):
        d, z = peer_n(i)
        remote(ps.at[z, d], pr.at[mz, md], p_s.at[z, d], p_r.at[mz, md], d, z).wait_send()

    each(dp, sent_d)
    each(fs, sent_z)
    each(n, sent_n)


def local(dp, fs, latents, targets, frozen_weight, adapter_down, adapter_up, categories, timesteps):
    _, _, rows, feat = latents.shape
    classes, rank, cols = adapter_down.shape
    fz = feat // fs
    hr, rz = rank // 2, rank // fs
    meta = jnp.concatenate([
        jnp.broadcast_to(categories[:, None], (1, 128)),
        jnp.broadcast_to(timesteps[:, None], (7, 128))], axis=0)
    vm = pl.BlockSpec(memory_space=pltpu.VMEM)
    dma = pltpu.SemaphoreType.DMA
    out = jax.ShapeDtypeStruct((classes, rank, cols), F32)
    gd, gu, loss = pl.pallas_call(
        functools.partial(kernel, dp, fs),
        out_shape=(out, out, jax.ShapeDtypeStruct((8, 128), F32)),
        in_specs=[vm] + [pl.BlockSpec(memory_space=pl.ANY)] * 5,
        out_specs=(vm,) * 3,
        scratch_shapes=[
            pltpu.VMEM((2 * rows, feat), BF16),
            pltpu.VMEM((2 * rows, feat), BF16),
            pltpu.VMEM((fz, feat), BF16),
            pltpu.VMEM((classes, rank, cols), BF16),
            pltpu.VMEM((classes, rank, cols), BF16),
            dma((5,)),
            pltpu.VMEM((dp, rank, 2 * cols), F32),
            pltpu.VMEM((dp, 8, 128), jnp.int32),
            pltpu.VMEM((dp, hr, 2 * cols), BF16),
            pltpu.VMEM((dp, hr, 2 * cols), BF16),
            pltpu.VMEM((dp, hr, 2 * cols), BF16),
            pltpu.VMEM((dp, hr, 2 * cols), BF16),
            pltpu.VMEM((rank, feat), BF16),
            pltpu.VMEM((rank, feat), BF16),
            pltpu.VMEM((fs, rank, fz), BF16),
            pltpu.VMEM((rank, feat), BF16),
            pltpu.VMEM((fs, rank, fz), BF16),
            pltpu.VMEM((fs, rank, fz), BF16),
            pltpu.VMEM((fs, 8, 128), F32),
            pltpu.VMEM((fs, dp, rz, 2 * cols), BF16),
            pltpu.VMEM((fs, dp, rz, 2 * cols), BF16),
            pltpu.VMEM((classes, rz, 2 * cols), F32),
            pltpu.VMEM((fs, classes, rz, 2 * cols), BF16),
            dma((dp,)), dma((dp,)), dma((dp,)), dma((dp,)), dma((dp,)), dma((dp,)),
            dma((fs,)), dma((fs,)), dma((fs,)), dma((fs,)), dma((fs,)), dma((fs,)),
            dma((fs, dp)), dma((fs, dp)), dma((fs,)), dma((fs,)),
        ],
        compiler_params=pltpu.CompilerParams(
            collective_id=0, has_side_effects=True, vmem_limit_bytes=56 * 1024 * 1024),
    )(meta, latents.reshape(2 * rows, feat), targets.reshape(2 * rows, feat),
      frozen_weight, adapter_down, adapter_up)
    return gd, gu, loss[0, 0:1]


def solution(mesh):
    placed = (
        P("dp", None, "fsdp", None),
        P("dp", None, "fsdp", None),
        P("fsdp", None),
        P(None, None, "dp"),
        P(None, None, "dp"),
        P("dp"),
        P("dp"),
    )
    return jax.shard_map(
        functools.partial(local, mesh.shape["dp"], mesh.shape["fsdp"]),
        mesh=mesh,
        in_specs=placed,
        out_specs=(P(None, None, "dp"), P(None, None, "dp"), P("dp")),
        check_vma=False,
    )
```

```python
import functools

import jax
import jax.numpy as jnp
from jax import lax
from jax.experimental import pallas as pl
from jax.experimental.pallas import tpu as pltpu
from jax.sharding import PartitionSpec as P

ADAPTER_SCALE = 0.5
BETA = 1.0
LOSS_SCALE = 64.0
F32 = jnp.float32
BF16 = jnp.bfloat16
MESH = pl.DeviceIdType.MESH


def dot(a, b, cb):
    return lax.dot_general(a, b, (((1,), (cb,)), ((), ())), preferred_element_type=F32)


def halves(a):
    high = a.astype(BF16)
    return high, (a - high.astype(F32)).astype(BF16)


def kernel(dp, fs, meta, x_in, t_in, w_in, ad_in, au_in, gd, gu, loss,
           x, t, w, ad, au, in_sem, pf, meta_all, us, ur, ds, dr, up, down, vr, vt, gs, gr, er, ps, pr, acc, orr,
           ms_s, ms_r, u_s, u_r, d_s, d_r, v_s, v_r, g_s, g_r, e_s, e_r, p_s, p_r, o_s, o_r):
    classes, rank, cols = ad.shape
    both_rows, feat = x.shape
    rows = both_rows // 2
    fz = feat // fs
    tokens = rows * fs
    hr = rank // 2
    rz = rank // fs
    n = dp * fs
    md, mz = lax.axis_index("dp"), lax.axis_index("fsdp")
    me = md * fs + mz

    def remote(src, dst, ss, rs, d, z):
        return pltpu.make_async_remote_copy(
            src_ref=src, dst_ref=dst, send_sem=ss, recv_sem=rs, device_id=(d, z), device_id_type=MESH)

    def each(count, body):
        def step(i, carry):
            body(i)
            return carry
        lax.fori_loop(1, count, step, 0)

    def peer_d(i):
        return lax.rem(md + i, dp)

    def peer_z(i):
        return lax.rem(mz + i, fs)

    def peer_n(i):
        lin = lax.rem(me + i, n)
        return lin // fs, lax.rem(lin, fs)

    loads = [pltpu.make_async_copy(src, dst, in_sem.at[i]) for i, (src, dst) in enumerate(
        ((au_in, au), (ad_in, ad), (w_in, w), (x_in, x), (t_in, t)))]
    for load in loads:
        load.start()

    barrier = pltpu.get_barrier_semaphore()

    def greet(i):
        d, z = peer_n(i)
        pl.semaphore_signal(barrier, inc=1, device_id=(d, z), device_id_type=MESH)

    each(n, greet)
    pl.semaphore_wait(barrier, n - 1)

    meta_all[md] = meta[...]
    each(dp, lambda i: remote(meta, meta_all.at[md], ms_s.at[i], ms_r.at[md], peer_d(i), mz).start())

    def meta_wait(i):
        d = peer_d(i)
        remote(meta, meta_all.at[d], ms_s.at[i], ms_r.at[d], d, mz).wait_recv()

    each(dp, meta_wait)

    def pick(source, d):
        cat = meta_all[d, 0:1, 0:1]
        out = jnp.zeros((rank, cols), F32)
        for c in range(classes):
            out = out + (cat == c).astype(F32) * source[c].astype(F32)
        return jnp.concatenate([out[:hr], out[hr:]], axis=1).astype(BF16)

    def send_part(source, sent, got, ss, rs):
        def body(i):
            d = peer_d(i)
            sent[d] = pick(source, d)
            remote(sent.at[d], got.at[md], ss.at[i], rs.at[md], d, mz).start()
        each(dp, body)
        got[md] = pick(source, md)

    loads[1].wait()
    send_part(ad, ds, dr, d_s, d_r)

    loads[0].wait()
    send_part(au, us, ur, u_s, u_r)

    def take_part(sent, got, ss, rs, whole):
        def body(i):
            d = peer_d(i)
            remote(sent.at[d], got.at[d], ss.at[i], rs.at[d], d, mz).wait_recv()
        each(dp, body)
        for d in range(dp):
            piece = got[d].astype(F32)
            whole[0:hr, cols * d:cols * (d + 1)] = piece[:, :cols].astype(BF16)
            whole[hr:rank, cols * d:cols * (d + 1)] = piece[:, cols:].astype(BF16)

    for load in loads[2:]:
        load.wait()
    take_part(ds, dr, d_s, d_r, down)
    ht = dot(down[...], x[...], 1).astype(BF16)
    sign = jnp.where(lax.broadcasted_iota(jnp.int32, (1, 2 * rows), 1) < rows, 1.0, -1.0).astype(F32)
    hf = ht.astype(F32)
    hts = (hf * sign).astype(BF16)
    g = dot(hts, x[...], 0)
    for z in range(fs):
        gs[z] = g[:, fz * z:fz * (z + 1)].astype(BF16)
    each(fs, lambda i: remote(gs.at[peer_z(i)], gr.at[mz], g_s.at[i], g_r.at[mz], md, peer_z(i)).start())
    gr[mz] = gs[mz]

    take_part(us, ur, u_s, u_r, up)
    v_exact = dot(w[...], up[...], 1).T
    v_half = v_exact.astype(BF16)
    vr[mz] = v_half
    each(fs, lambda i: remote(vr.at[mz], vr.at[mz], v_s.at[i], v_r.at[mz], md, peer_z(i)).start())

    uu_h, uu_l = halves(dot(up[...], up[...], 1))
    huu = ADAPTER_SCALE * (dot(uu_h, ht, 0) + dot(uu_l, ht, 0))
    st = huu - dot(up[...], t[...], 1)
    m_h, m_l = halves(ADAPTER_SCALE * dot(hts, ht, 1))
    pu = dot(m_h, up[...], 0) + dot(m_l, up[...], 0) - dot(hts, t[...], 0)

    def g_wait(i):
        z = peer_z(i)
        remote(gs.at[z], gr.at[z], g_s.at[i], g_r.at[z], md, z).wait_recv()

    each(fs, g_wait)
    g_wide = gr[0].astype(F32)
    for z in range(1, fs):
        g_wide = g_wide + gr[z].astype(F32)
    g_h, g_l = halves(g_wide)
    pu = pu + dot(g_h, w[...], 0) + dot(g_l, w[...], 0)

    def v_wait(i):
        z = peer_z(i)
        remote(vr.at[z], vr.at[z], v_s.at[i], v_r.at[z], md, z).wait_recv()

    each(fs, v_wait)
    for z in range(fs):
        vt[:, fz * z:fz * (z + 1)] = vr[z]
    st = st + dot(vt[...], x[...], 1)

    err = jnp.sum(sign * (ADAPTER_SCALE * hf * (2.0 * st - huu)), axis=(0, 1), keepdims=True)
    err = err + 2.0 * ADAPTER_SCALE * jnp.sum(
        g_wide * (v_exact - v_half.astype(F32)), axis=(0, 1), keepdims=True)
    er[mz] = jnp.broadcast_to(err, (8, 128))
    each(fs, lambda i: remote(er.at[mz], er.at[mz], e_s.at[i], e_r.at[mz], md, peer_z(i)).start())

    back = (st * sign).astype(BF16)
    pd = dot(back, x[...], 0)
    for d in range(dp):
        pf[d] = jnp.concatenate(
            [pd[:, cols * d:cols * (d + 1)], pu[:, cols * d:cols * (d + 1)]], axis=1)

    def e_wait(i):
        z = peer_z(i)
        remote(er.at[z], er.at[z], e_s.at[i], e_r.at[z], md, z).wait_recv()

    each(fs, e_wait)
    diff = er[0]
    for z in range(1, fs):
        diff = diff + er[z]
    diff = diff[0:1, :] / tokens
    my_cat = meta[0:1, :]
    kappa = BETA * (0.5 + meta[1:2, :].astype(F32) / 1000.0)
    zvalue = kappa * diff
    decay = jnp.exp(-jnp.abs(zvalue))
    loss[...] = jnp.broadcast_to(jnp.maximum(zvalue, 0.0) + jnp.log1p(decay), (8, 128))
    total = lax.fori_loop(
        0, dp, lambda d, s: s + (meta_all[d, 0:1, :] == my_cat).astype(F32), jnp.zeros((1, 128), F32))
    sigmoid = jnp.where(zvalue >= 0.0, 1.0, decay) / (1.0 + decay)
    scale = (ADAPTER_SCALE * 2.0 * LOSS_SCALE / tokens) * kappa * sigmoid / total

    for d in range(dp):
        joined = (pf[d] * scale[:, 0:1]).astype(BF16)
        for z in range(fs):
            ps[z, d] = joined[rz * z:rz * (z + 1)]

    def p_send(i):
        d, z = peer_n(i)
        remote(ps.at[z, d], pr.at[mz, md], p_s.at[z, d], p_r.at[mz, md], d, z).start()

    def p_wait(d, z):
        remote(ps.at[z, d], pr.at[z, d], p_s.at[z, d], p_r.at[z, d], d, z).wait_recv()

    each(n, p_send)
    pr[mz, md] = ps[mz, md]
    acc[...] = jnp.zeros_like(acc)

    def gather(d, carry):
        piece = pr[0, d].astype(F32)
        for z in range(1, fs):
            piece = piece + pr[z, d].astype(F32)
        cat = meta_all[d, 0:1, 0:1]
        for c in range(classes):
            acc[c] += (cat == c).astype(F32) * piece
        return carry

    each(fs, lambda i: p_wait(md, peer_z(i)))
    gather(md, 0)

    def p_take(i):
        d = lax.rem(md + dp - i, dp)
        for z in range(fs):
            p_wait(d, z)
        gather(d, 0)

    each(dp, p_take)
    orr[mz] = acc[...].astype(BF16)
    each(fs, lambda i: remote(orr.at[mz], orr.at[mz], o_s.at[i], o_r.at[mz], md, peer_z(i)).start())

    def o_wait(i):
        z = peer_z(i)
        remote(orr.at[z], orr.at[z], o_s.at[i], o_r.at[z], md, z).wait_recv()

    each(fs, o_wait)
    for z in range(fs):
        part = orr[z].astype(F32)
        gd[:, rz * z:rz * (z + 1), :] = part[:, :, :cols]
        gu[:, rz * z:rz * (z + 1), :] = part[:, :, cols:]

    def sent_d(i):
        d = peer_d(i)
        remote(meta, meta_all.at[md], ms_s.at[i], ms_r.at[md], d, mz).wait_send()
        remote(us.at[d], ur.at[md], u_s.at[i], u_r.at[md], d, mz).wait_send()
        remote(ds.at[d], dr.at[md], d_s.at[i], d_r.at[md], d, mz).wait_send()

    def sent_z(i):
        z = peer_z(i)
        remote(vr.at[mz], vr.at[mz], v_s.at[i], v_r.at[mz], md, z).wait_send()
        remote(gs.at[z], gr.at[mz], g_s.at[i], g_r.at[mz], md, z).wait_send()
        remote(er.at[mz], er.at[mz], e_s.at[i], e_r.at[mz], md, z).wait_send()
        remote(orr.at[mz], orr.at[mz], o_s.at[i], o_r.at[mz], md, z).wait_send()

    def sent_n(i):
        d, z = peer_n(i)
        remote(ps.at[z, d], pr.at[mz, md], p_s.at[z, d], p_r.at[mz, md], d, z).wait_send()

    each(dp, sent_d)
    each(fs, sent_z)
    each(n, sent_n)


def local(dp, fs, latents, targets, frozen_weight, adapter_down, adapter_up, categories, timesteps):
    _, _, rows, feat = latents.shape
    classes, rank, cols = adapter_down.shape
    fz = feat // fs
    hr, rz = rank // 2, rank // fs
    meta = jnp.concatenate([
        jnp.broadcast_to(categories[:, None], (1, 128)),
        jnp.broadcast_to(timesteps[:, None], (7, 128))], axis=0)
    vm = pl.BlockSpec(memory_space=pltpu.VMEM)
    dma = pltpu.SemaphoreType.DMA
    out = jax.ShapeDtypeStruct((classes, rank, cols), F32)
    gd, gu, loss = pl.pallas_call(
        functools.partial(kernel, dp, fs),
        out_shape=(out, out, jax.ShapeDtypeStruct((8, 128), F32)),
        in_specs=[vm] + [pl.BlockSpec(memory_space=pl.ANY)] * 5,
        out_specs=(vm,) * 3,
        scratch_shapes=[
            pltpu.VMEM((2 * rows, feat), BF16),
            pltpu.VMEM((2 * rows, feat), BF16),
            pltpu.VMEM((fz, feat), BF16),
            pltpu.VMEM((classes, rank, cols), BF16),
            pltpu.VMEM((classes, rank, cols), BF16),
            dma((5,)),
            pltpu.VMEM((dp, rank, 2 * cols), F32),
            pltpu.VMEM((dp, 8, 128), jnp.int32),
            pltpu.VMEM((dp, hr, 2 * cols), BF16),
            pltpu.VMEM((dp, hr, 2 * cols), BF16),
            pltpu.VMEM((dp, hr, 2 * cols), BF16),
            pltpu.VMEM((dp, hr, 2 * cols), BF16),
            pltpu.VMEM((rank, feat), BF16),
            pltpu.VMEM((rank, feat), BF16),
            pltpu.VMEM((fs, rank, fz), BF16),
            pltpu.VMEM((rank, feat), BF16),
            pltpu.VMEM((fs, rank, fz), BF16),
            pltpu.VMEM((fs, rank, fz), BF16),
            pltpu.VMEM((fs, 8, 128), F32),
            pltpu.VMEM((fs, dp, rz, 2 * cols), BF16),
            pltpu.VMEM((fs, dp, rz, 2 * cols), BF16),
            pltpu.VMEM((classes, rz, 2 * cols), F32),
            pltpu.VMEM((fs, classes, rz, 2 * cols), BF16),
            dma((dp,)), dma((dp,)), dma((dp,)), dma((dp,)), dma((dp,)), dma((dp,)),
            dma((fs,)), dma((fs,)), dma((fs,)), dma((fs,)), dma((fs,)), dma((fs,)),
            dma((fs, dp)), dma((fs, dp)), dma((fs,)), dma((fs,)),
        ],
        compiler_params=pltpu.CompilerParams(
            collective_id=0, has_side_effects=True, vmem_limit_bytes=56 * 1024 * 1024),
    )(meta, latents.reshape(2 * rows, feat), targets.reshape(2 * rows, feat),
      frozen_weight, adapter_down, adapter_up)
    return gd, gu, loss[0, 0:1]


def solution(mesh):
    placed = (
        P("dp", None, "fsdp", None),
        P("dp", None, "fsdp", None),
        P("fsdp", None),
        P(None, None, "dp"),
        P(None, None, "dp"),
        P("dp"),
        P("dp"),
    )
    return jax.shard_map(
        functools.partial(local, mesh.shape["dp"], mesh.shape["fsdp"]),
        mesh=mesh,
        in_specs=placed,
        out_specs=(P(None, None, "dp"), P(None, None, "dp"), P("dp")),
        check_vma=False,
    )
```
